32 devices in a mesh: leaf: 32 (over z, y, x, core).
Axes of the slice: x: 2, y: 2, z: 4, core: 2. Of those that a mesh axis runs over, the one named last changes fastest.
Arguments:
- x_vecs: bfloat16 [16, 262144], P(None, 'leaf'), may hold values from -6 to 6
- leaf_basis: bfloat16 [4096, 4096], P('leaf'), may hold values from -0.75 to 0.75
- near_blocks: bfloat16 [4096, 12288], P('leaf'), may hold values from -0.4375 to 0.4375
- local_edges: float32 [8128, 4096], P('leaf'), may hold values from -0.5 to 0.5
- top_edges: float32 [32, 4, 4096], P('leaf'), may hold values from -1 to 1, as said below
- top_couple: float32 [32, 5, 4096], P('leaf'), may hold values from -3 to 3, as said below
- couple_blocks: bfloat16 [16384, 4096], P('leaf'), may hold values from -0.75 to 0.75
- couple_src: int32 [16384], P('leaf'), may hold values from 0 to 127
- couple_owner: int32 [16384, 1], P('leaf'), may hold values from 0 to 31; in each aligned block of 512 rows (0 to 511, 512 to 1023, ...) at most 32 rows name the same one
- couple_dst: int32 [16384], P('leaf'), may hold values from 0 to 127
Outputs:
- y_vecs: float32 [16, 262144], P(None, 'leaf')
The draws below stay inside these ranges and needn't reach their ends.
Inputs may be any that keep to these rules, and one draw needn't show every extreme that they name: `couple_owner`: the rows of one device name each owner at most 32 times, a bound that some block reaches. top_edges[o, b] belongs to the level-b cluster that holds device o and is the same for all devices of that cluster. top_couple[o, b] belongs to the level-b cluster that holds device o and is the same for all devices of that cluster.
All inputs are finite; a program needn't handle non-finite values.
Results may differ from the reference program's by a relative error of at most 0.0044.
Values may be sent and summed in bfloat16 or wider, within the bound.
A program may use at most 128 MiB of HBM per device.

```python
import math
import jax
import jax.numpy as jnp
import numpy as np
from jax import lax

LEAF = 64
RANK = 64
NV = 16
LEAF_DEV = 128
OWNERS = 32
TOPLV = 5
TOPE = 4
LEAVES = 4096
POINTS = 262144
EDGES = 8128
PAIRS_DEV = 512
PAIRS = 16384
CAP = 32


def spread_levels(key, depth_count, spread):
    raw_values = jnp.clip(jax.random.normal(key, (OWNERS, depth_count, RANK * RANK), jnp.float32), -3.0, 3.0) * spread
    owner_ids = jnp.arange(OWNERS, dtype=jnp.int32)
    columns = []
    for depth in range(depth_count):
        leading = owner_ids // 2 ** depth * 2 ** depth
        columns.append(raw_values[leading, depth])
    return jnp.stack(columns, axis=1)


def draw_top_edges(key, part):
    return spread_levels(jax.random.fold_in(key, 11), TOPE, (2.0 * RANK) ** (-0.5))


def draw_top_couple(key, part):
    return spread_levels(jax.random.fold_in(key, 23), TOPLV, 3.0 * RANK ** (-0.5))


def with_ends(array, key, smallest, largest):
    place = [jax.random.randint(jax.random.fold_in(key, axis), (), 0, length) for axis, length in enumerate(array.shape)]
    main_axis = array.shape.index(max(array.shape))
    beside = place[:main_axis] + [(place[main_axis] + 1) % array.shape[main_axis]] + place[main_axis + 1:]
    return array.at[tuple(place)].set(smallest).at[tuple(beside)].set(largest)


def shard_levels(stream_key, shape, shards, least, largest):
    gain, own = 1.0, jax.random.fold_in(stream_key, 6)
    for dim, parts in shards:
        heights = jnp.exp(jax.random.uniform(jax.random.fold_in(own, dim), (parts,), jnp.float32, least / len(shards), largest / len(shards)))
        gain = gain * jnp.repeat(heights, shape[dim] // parts).reshape([-1 if axis == dim else 1 for axis in range(len(shape))])
    return gain


def assign_block(key, own, number, rows, amount, top, limit, skew):
    sequence = jax.random.permutation(key, amount)
    packed, ordinary = portions_of(amount, rows * top, limit, skew, True), portions_of(amount, rows * top, limit, skew, False)
    places = jnp.arange(amount)

    def named(lengths, turn):
        used = int((lengths > 0).sum())
        fixed = max(1, used // 4)
        passed = fixed + (places - fixed + turn * (used - fixed)) % max(1, amount - fixed)
        return jnp.zeros((amount,), jnp.int32).at[sequence[jnp.where(places < fixed, places, passed)]].set(jnp.asarray(lengths, jnp.int32))

    lengths = jnp.where(number % 4 == 0, named(packed, number // 4), named(ordinary, number - number // 4 - 1))
    mixed = jax.random.permutation(jax.random.fold_in(own, 3), amount)
    donor, taker = mixed[0:amount // 2 * 2:2], mixed[1:amount // 2 * 2:2]
    margin = jnp.minimum(lengths[donor] - 1, limit - lengths[taker]) // 2
    margin = jnp.where((donor == sequence[0]) | (taker == sequence[0]) | (lengths[taker] == 0), 0, jnp.maximum(margin, 0))
    passed = jax.random.randint(jax.random.fold_in(own, 4), (amount // 2,), 0, 1 << 20) % (margin + 1)
    lengths = lengths.at[donor].add(-passed).at[taker].add(passed)
    labels = jnp.searchsorted(jnp.cumsum(lengths), jnp.arange(rows * top), side="right").astype(jnp.int32)
    table = labels.reshape(top, rows).T
    table = table[jax.random.permutation(jax.random.fold_in(own, 1), rows)]
    turn = jax.random.randint(jax.random.fold_in(own, 2), (rows, 1), 0, top)
    return jnp.take_along_axis(table, (jnp.arange(top)[None, :] + turn) % top, axis=1)


def portions_of(amount, total, limit, slope, full):
    weights = [(1 << 20) // math.isqrt(rank ** slope) + 1 for rank in range(1, amount + 1)]
    largest = limit if full else min(limit, max(-(-total // amount), total * weights[0] // sum(weights)))
    least = 1 if total - largest >= amount - 1 else 0
    holding, surplus = [largest] + [least] * (amount - 1), total - largest - least * (amount - 1)
    while surplus > 0:
        movable = [i for i in range(1, amount) if holding[i] < largest] or [i for i in range(1, amount) if holding[i] < limit]
        whole, left = sum([weights[i] for i in movable]), surplus
        for i in movable:
            addition = min(limit - holding[i], max(1, left * weights[i] // whole), surplus)
            holding[i] = holding[i] + addition
            surplus = surplus - addition
    return np.array(holding)


def bell_draw(rng, shape, deviation, most, pieces=(), kind=jnp.bfloat16):
    loudness = shard_levels(rng, shape, pieces, -0.22, 0.18) if pieces else 1.0
    drawn = jax.random.normal(rng, shape, jnp.float32) * deviation * loudness
    return jnp.minimum(jnp.maximum(drawn, -most), most).astype(kind)


def setup_inputs(seed: int = 0) -> dict:
    streams_of = jax.random.split(jax.random.key(seed), 11)
    x_vecs = bell_draw(streams_of[0], (NV, POINTS), 1.0, 6.0, ((1, 32),))
    leaf_basis = bell_draw(streams_of[1], (LEAVES, LEAF * RANK), LEAF ** -0.5, 0.75, ((0, 32),))
    near_blocks = bell_draw(streams_of[2], (LEAVES, 3 * LEAF * LEAF), (3 * LEAF) ** -0.5, 0.4375, ((0, 32),))
    local_edges = bell_draw(streams_of[3], (EDGES, RANK * RANK), (2 * RANK) ** -0.5, 0.5, ((0, 32),), jnp.float32)
    top_edges = draw_top_edges(jax.random.fold_in(streams_of[10], 71), 0)
    top_couple = draw_top_couple(jax.random.fold_in(streams_of[10], 71), 0)
    couple_blocks = bell_draw(streams_of[6], (PAIRS, RANK * RANK), RANK ** -0.5, 0.75, ((0, 32),))
    couple_src = with_ends(jax.random.randint(streams_of[7], (PAIRS,), 0, LEAF_DEV), jax.random.fold_in(streams_of[7], 1), 0, LEAF_DEV - 1).astype(jnp.int32)
    couple_owner_keys = jax.random.split(jax.random.fold_in(streams_of[8], 1), PAIRS // PAIRS_DEV)
    couple_owner_turns = jax.random.permutation(jax.random.fold_in(streams_of[8], 3), PAIRS // PAIRS_DEV)
    couple_owner = jax.vmap(lambda own, number: assign_block(jax.random.fold_in(streams_of[8], 2), own, number, PAIRS_DEV, OWNERS, 1, CAP, 2))(couple_owner_keys, couple_owner_turns).reshape((PAIRS, 1))
    couple_dst = with_ends(jax.random.randint(streams_of[9], (PAIRS,), 0, LEAF_DEV), jax.random.fold_in(streams_of[9], 1), 0, LEAF_DEV - 1).astype(jnp.int32)
    return {"x_vecs": x_vecs, "leaf_basis": leaf_basis, "near_blocks": near_blocks, "local_edges": local_edges, "top_edges": top_edges, "top_couple": top_couple, "couple_blocks": couple_blocks, "couple_src": couple_src, "couple_owner": couple_owner, "couple_dst": couple_dst}


exact_prec = lax.Precision.HIGHEST


def reference(x_vecs, leaf_basis, near_blocks, local_edges, top_edges, top_couple, couple_blocks, couple_src, couple_owner, couple_dst):
    vec_leaves = x_vecs.reshape(NV, LEAVES, LEAF).astype(jnp.float32)
    bases_all = leaf_basis.reshape(LEAVES, LEAF, RANK).astype(jnp.float32)
    coeffs = jnp.einsum('vtp,tpk->tvk', vec_leaves, bases_all)
    coeff_round = coeffs.astype(jnp.bfloat16)
    edge_mats = local_edges.reshape(OWNERS, 2 * LEAF_DEV - 2, RANK, RANK)
    states = coeffs.reshape(OWNERS, LEAF_DEV, NV, RANK)
    offset = 0
    nodes_now = LEAF_DEV
    while nodes_now > 1:
        chosen = edge_mats[:, offset:offset + nodes_now]
        carried = jnp.einsum('onvk,onkl->onvl', states, chosen, precision=exact_prec)
        carried = carried.reshape(OWNERS, nodes_now // 2, 2, NV, RANK)
        states = carried[:, :, 0] + carried[:, :, 1]
        offset = offset + nodes_now
        nodes_now = nodes_now // 2
    root_coeff = states[:, 0]
    top_coeff = [root_coeff]
    for section_no in range(TOPLV - 1):
        stride = 2 ** section_no
        chosen = top_edges[::stride, section_no].reshape(-1, RANK, RANK)
        carried = jnp.einsum('mvk,mkl->mvl', top_coeff[-1], chosen, precision=exact_prec)
        carried = carried.reshape(-1, 2, NV, RANK)
        top_coeff.append(carried[:, 0] + carried[:, 1])
    top_down = jnp.zeros((1, NV, RANK), jnp.float32)
    for section_no in reversed(range(TOPLV)):
        stride = 2 ** section_no
        current = top_coeff[section_no]
        nodes_here = current.shape[0]
        sibling = current.reshape(nodes_here // 2, 2, NV, RANK)[:, ::-1].reshape(nodes_here, NV, RANK)
        coupling = top_couple[::stride, section_no].reshape(nodes_here, RANK, RANK)
        result = jnp.einsum('mvl,mkl->mvk', sibling, coupling, precision=exact_prec)
        if section_no < TOPLV - 1:
            parent = jnp.repeat(top_down, 2, axis=0)
            chosen = top_edges[::stride, section_no].reshape(nodes_here, RANK, RANK)
            result = result + jnp.einsum('mvl,mkl->mvk', parent, chosen, precision=exact_prec)
        top_down = result
    states = top_down[:, None]
    nodes_now = 1
    while nodes_now < LEAF_DEV:
        nodes_now = nodes_now * 2
        offset = 2 * LEAF_DEV - 2 * nodes_now
        chosen = edge_mats[:, offset:offset + nodes_now]
        parent = jnp.repeat(states, 2, axis=1)
        states = jnp.einsum('onvl,onkl->onvk', parent, chosen, precision=exact_prec)
    leaf_down = states.reshape(LEAVES, NV, RANK)
    pair_ids = jnp.arange(PAIRS, dtype=jnp.int32)
    src_global = (pair_ids // PAIRS_DEV) * LEAF_DEV + couple_src
    dst_global = couple_owner[:, 0] * LEAF_DEV + couple_dst
    picked = coeff_round[src_global].astype(jnp.float32)
    pair_mats = couple_blocks.reshape(PAIRS, RANK, RANK).astype(jnp.float32)
    pair_round = jnp.einsum('pvl,pkl->pvk', picked, pair_mats).astype(jnp.bfloat16)
    pair_round = lax.optimization_barrier(pair_round)
    far_sum = jax.ops.segment_sum(pair_round.astype(jnp.float32), dst_global, num_segments=LEAVES)
    leaf_hat = (leaf_down + far_sum).astype(jnp.bfloat16)
    blocks = near_blocks.reshape(LEAVES, 3, LEAF, LEAF).astype(jnp.float32)
    before = jnp.roll(vec_leaves, 1, axis=1)
    following = jnp.roll(vec_leaves, -1, axis=1)
    near_part = jnp.einsum('vtq,tpq->vtp', before, blocks[:, 0])
    near_part = near_part + jnp.einsum('vtq,tpq->vtp', vec_leaves, blocks[:, 1])
    near_part = near_part + jnp.einsum('vtq,tpq->vtp', following, blocks[:, 2])
    far_part = jnp.einsum('tvk,tpk->vtp', leaf_hat.astype(jnp.float32), bases_all)
    return (far_part + near_part).reshape(NV, POINTS)
```

```python
import functools

import jax
import jax.numpy as jnp
from jax import lax
from jax.experimental import pallas as pl
from jax.experimental.pallas import tpu as pltpu
from jax.sharding import PartitionSpec as P

LEAF = 64
RANK = 64
NV = 16
LEAF_DEV = 128
GROUP = 16
ROWS = GROUP * NV

exact_prec = lax.Precision.HIGHEST
f32 = jnp.float32
bf16 = jnp.bfloat16
CP = pltpu.CompilerParams(vmem_limit_bytes=56 * 2**20)
VM = pl.BlockSpec(memory_space=pltpu.VMEM)
SM = pl.BlockSpec(memory_space=pltpu.SMEM)


def partner(value, axis, distance):
    mask = 2**distance
    pairs = [(source, source ^ mask) for source in range(lax.axis_size(axis))]
    return lax.ppermute(value, axis, pairs)


def spread_const():
    row = lax.broadcasted_iota(jnp.int32, (RANK, 1024), 0)
    lane = lax.broadcasted_iota(jnp.int32, (RANK, 1024), 1)
    want = (lane // 512) * 32 + (lane // 256) % 2 + 2 * ((lane % 256) // GROUP)
    return jnp.where(row == want, 1.0, 0.0).astype(bf16)


def group_mask(rows, first):
    row = lax.broadcasted_iota(jnp.int32, (rows, ROWS), 0)
    lane = lax.broadcasted_iota(jnp.int32, (rows, ROWS), 1)
    return jnp.where(row // NV + first == lane % GROUP, 1.0, 0.0)


def stack(rows, half):
    return jnp.concatenate(
        [rows[:, (16 * half + j) * 128 : (16 * half + j + 1) * 128] for j in range(16)], axis=0
    )


def split(value):
    high = value.astype(bf16)
    return high, (value - high.astype(f32)).astype(bf16)


def dot(a, b):
    return jnp.dot(a, b, preferred_element_type=f32)


def dot_t(a, b):
    return lax.dot_general(a, b, (((1,), (1,)), ((), ())), preferred_element_type=f32)


def times(terms, spread, mask):
    mask = mask.astype(bf16)
    total = [None, None]
    for c, stacks in terms:
        wide = dot(c, spread).astype(bf16)
        for h in range(2):
            for par in range(2):
                at = (2 * h + par) * 256
                left = wide[:, at : at + 256] * mask
                for rows in stacks:
                    part = dot(left, rows[h])
                    total[par] = part if total[par] is None else total[par] + part
    return total[0][:, :RANK] + total[1][:, RANK:]


def times_t_wide(terms):
    out = [[None, None], [None, None]]
    for c, stacks in terms:
        zero = jnp.zeros_like(c)
        for par in range(2):
            left = jnp.concatenate([c, zero] if par == 0 else [zero, c], axis=1)
            for rows in stacks:
                for h in range(2):
                    part = dot_t(left, rows[h])
                    out[par][h] = part if out[par][h] is None else out[par][h] + part
    return out


def pick_own(wide, spread, mask, exact):
    total = None
    for par in range(2):
        for h in range(2):
            at = (2 * h + par) * 256
            sel = spread[:, at : at + 256]
            if exact:
                parts = split(wide[par][h] * mask)
            else:
                parts = [wide[par][h].astype(bf16) * mask.astype(bf16)]
            for piece in parts:
                part = dot_t(piece, sel)
                total = part if total is None else total + part
    return total


def edge_stacks(e_ref, first, count):
    rows = e_ref[pl.ds(first, count), :]
    if count < GROUP:
        rows = jnp.concatenate([rows, jnp.zeros((GROUP - count, 4096), f32)], axis=0)
    high, low = split(rows)
    return [stack(high, h) for h in range(2)], [stack(low, h) for h in range(2)]


def up_kernel(x_ref, u_ref, e_ref, c_ref, root_ref, xs, state, spread_ref):
    spread_ref[...] = spread_const()
    for i in range(LEAF_DEV // 2):
        blk = x_ref[:, 128 * i : 128 * i + 128]
        xs[32 * i : 32 * i + 16, :] = blk[:, :64]
        xs[32 * i + 16 : 32 * i + 32, :] = blk[:, 64:]
    mask = group_mask(ROWS, 0)

    def leaf_step(g, carry):
        u = u_ref[pl.ds(pl.multiple_of(g * GROUP, GROUP), GROUP), :]
        at = pl.multiple_of(g * ROWS, ROWS)
        c = times([(xs[pl.ds(at, ROWS), :], [[stack(u, 0), stack(u, 1)]])], spread_ref[...], mask)
        c_ref[pl.ds(at, ROWS), :] = c.astype(bf16)
        state[pl.ds(at, ROWS), :] = c
        return carry

    lax.fori_loop(0, LEAF_DEV // GROUP, leaf_step, 0)

    def climb(c, stacks, m):
        hi, lo = stacks
        c_hi, c_lo = split(c)
        out = times([(c_hi, [hi, lo]), (c_lo, [hi])], spread_ref[...], m)
        n = c.shape[0] // NV
        out = out.reshape(n // 2, 2, NV, RANK)
        return (out[:, 0] + out[:, 1]).reshape(n // 2 * NV, RANK)

    offset = 0
    nodes = LEAF_DEV
    while nodes >= GROUP:

        def step(g, carry, offset=offset):
            at = pl.multiple_of(g * ROWS, ROWS)
            to = pl.multiple_of(g * (ROWS // 2), ROWS // 2)
            stacks = edge_stacks(e_ref, pl.multiple_of(offset + g * GROUP, GROUP), GROUP)
            state[pl.ds(to, ROWS // 2), :] = climb(state[pl.ds(at, ROWS), :], stacks, mask)
            return carry

        if nodes == GROUP:
            step(0, 0)
        else:
            lax.fori_loop(0, nodes // GROUP, step, 0)
        offset += nodes
        nodes //= 2
    stacks = edge_stacks(e_ref, offset, 14)
    c = state[0 : ROWS // 2, :]
    first = 0
    while c.shape[0] > NV:
        rows = c.shape[0]
        c = climb(c, stacks, group_mask(rows, first))
        first += rows // NV
    root_ref[...] = c


def pair_kernel(cap, src, slot, c_ref, m_ref, t_ref, out_ref, buf, spread_ref):
    spread_ref[...] = spread_const()
    buf[...] = jnp.zeros_like(buf)
    mask = group_mask(ROWS, 0)

    def step(g, carry):
        m = m_ref[pl.ds(pl.multiple_of(g * GROUP, GROUP), GROUP), :]
        c = jnp.concatenate(
            [c_ref[pl.ds(pl.multiple_of(src[g * GROUP + i] * NV, NV), NV), :] for i in range(GROUP)],
            axis=0,
        )
        wide = times_t_wide([(c, [[stack(m, 0), stack(m, 1)]])])
        got = pick_own(wide, spread_ref[...], mask, False)
        for i in range(GROUP):
            block = got[i * NV : (i + 1) * NV, :]
            packed = jnp.concatenate([block[:8], block[8:]], axis=1)
            buf[pl.ds(pl.multiple_of(slot[g * GROUP + i] * 8, 8), 8), :] = packed
        return carry

    lax.fori_loop(0, m_ref.shape[0] // GROUP, step, 0)
    per = cap * 8
    for p in range(out_ref.shape[0]):
        out_ref[p, 0:per, :] = buf[p * per : (p + 1) * per, :].astype(bf16)
        out_ref[p, per : per + 16, :] = t_ref[p]


def down_kernel(hat_ref, e_ref, x_ref, low_ref, high_ref, n_ref, down_ref, near_ref, xs, spread_ref):
    spread_ref[...] = spread_const()
    mask = group_mask(ROWS, 0)
    leaves = LEAF_DEV
    xs[0:NV, :] = low_ref[...]
    xs[NV + leaves * NV : 2 * NV + leaves * NV, :] = high_ref[...]
    for i in range(leaves // 2):
        blk = x_ref[:, 128 * i : 128 * i + 128]
        xs[NV + 32 * i : NV + 32 * i + 16, :] = blk[:, :64]
        xs[NV + 32 * i + 16 : NV + 32 * i + 32, :] = blk[:, 64:]

    def near_step(g, carry):
        at = pl.multiple_of(g * ROWS, ROWS)
        terms = []
        for d in range(3):
            m = n_ref[pl.ds(pl.multiple_of(g * GROUP, GROUP), GROUP), d * 4096 : (d + 1) * 4096]
            c = xs[pl.ds(pl.multiple_of(at + d * NV, NV), ROWS), :]
            terms.append((c, [[stack(m, 0), stack(m, 1)]]))
        near_ref[pl.ds(at, ROWS), :] = pick_own(times_t_wide(terms), spread_ref[...], mask, True)
        return carry

    lax.fori_loop(0, leaves // GROUP, near_step, 0)

    def fall(c, stacks, m):
        n = c.shape[0] // NV
        c = jnp.broadcast_to(c.reshape(n, 1, NV, RANK), (n, 2, NV, RANK)).reshape(2 * n * NV, RANK)
        hi, lo = stacks
        c_hi, c_lo = split(c)
        wide = times_t_wide([(c_hi, [hi, lo]), (c_lo, [hi])])
        return pick_own(wide, spread_ref[...], m, True)

    stacks = edge_stacks(e_ref, 2 * LEAF_DEV - 16, 14)
    c = hat_ref[...]
    for nodes in (2, 4, 8):
        c = fall(c, stacks, group_mask(nodes * NV, 16 - 2 * nodes))
    nodes = 16
    down_ref[0 : 8 * NV, :] = c
    while nodes <= LEAF_DEV:
        offset = 2 * LEAF_DEV - 2 * nodes
        groups = nodes // GROUP

        def step(i, carry, offset=offset, groups=groups):
            g = groups - 1 - i
            at = pl.multiple_of(g * (ROWS // 2), ROWS // 2)
            to = pl.multiple_of(g * ROWS, ROWS)
            stacks = edge_stacks(e_ref, pl.multiple_of(offset + g * GROUP, GROUP), GROUP)
            down_ref[pl.ds(to, ROWS), :] = fall(down_ref[pl.ds(at, ROWS // 2), :], stacks, mask)
            return carry

        if groups == 1:
            step(0, 0)
        else:
            lax.fori_loop(0, groups, step, 0)
        nodes *= 2


def final_kernel(tgt, arr_ref, down_ref, near_ref, u_ref, y_ref, acc0, acc1, acc2, acc3, spread_ref):
    spread_ref[...] = spread_const()
    mask = group_mask(ROWS, 0)
    accs = (acc0, acc1, acc2, acc3)
    for a in accs:
        a[...] = jnp.zeros_like(a)
    peers, per, _ = arr_ref.shape
    cap = (per - 16) // 8

    def land(p, carry):
        for q in range(cap // 2):
            pair = arr_ref[p, 16 * q : 16 * q + 16, :].astype(f32)
            for i in range(2):
                a = accs[(2 * q + i) % 4]
                t = tgt[p * cap + 2 * q + i]
                at = pl.ds(pl.multiple_of(t * 8, 8), 8)
                a[at, :] = a[at, :] + pair[8 * i : 8 * i + 8, :]
        return carry

    lax.fori_loop(0, peers, land, 0)

    for g in range(LEAF_DEV // GROUP):
        part = slice(g * 128, (g + 1) * 128)
        far = (acc0[part, :] + acc1[part, :]) + (acc2[part, :] + acc3[part, :])
        rows = []
        for t in range(GROUP):
            block = far[8 * t : 8 * t + 8, :]
            rows += [block[:, :64], block[:, 64:]]
        far = jnp.concatenate(rows, axis=0)
        own = slice(g * ROWS, (g + 1) * ROWS)
        hat = (down_ref[own, :] + far).astype(bf16)
        u = u_ref[g * GROUP : (g + 1) * GROUP, :]
        wide = times_t_wide([(hat, [[stack(u, 0), stack(u, 1)]])])
        y = pick_own(wide, spread_ref[...], mask, True) + near_ref[own, :]
        for i in range(GROUP // 2):
            left = y[32 * i : 32 * i + 16, :]
            right = y[32 * i + 16 : 32 * i + 32, :]
            at = (g * GROUP // 2 + i) * 128
            y_ref[:, at : at + 128] = jnp.concatenate([left, right], axis=1)


def shards(
    x_vecs,
    leaf_basis,
    near_blocks,
    local_edges,
    top_edges,
    top_couple,
    couple_blocks,
    couple_src,
    couple_owner,
    couple_dst,
):
    leaf_count = leaf_basis.shape[0]
    peer_count = lax.axis_size("leaf")
    pair_count = couple_blocks.shape[0]
    spread_shape = pltpu.VMEM((RANK, 1024), bf16)
    points = leaf_count * NV

    coeff_round, root_coeff = pl.pallas_call(
        up_kernel,
        out_shape=(
            jax.ShapeDtypeStruct((points, RANK), bf16),
            jax.ShapeDtypeStruct((NV, RANK), f32),
        ),
        in_specs=[VM] * 3,
        out_specs=(VM, VM),
        scratch_shapes=[
            pltpu.VMEM((points, RANK), bf16),
            pltpu.VMEM((points, RANK), f32),
            spread_shape,
        ],
        compiler_params=CP,
        name="up",
    )(x_vecs, leaf_basis, local_edges)

    slot_cap = max(4, 2 * ((pair_count + peer_count - 1) // peer_count))
    slot_total = peer_count * slot_cap
    owners = couple_owner[:, 0]
    onehot = (owners[:, None] == jnp.arange(peer_count, dtype=jnp.int32)[None, :]).astype(jnp.int32)
    slot_rank = jnp.sum((jnp.cumsum(onehot, axis=0) - onehot) * onehot, axis=1)
    slot_ids = owners * slot_cap + slot_rank
    placing = slot_ids[None, :] == jnp.arange(slot_total, dtype=jnp.int32)[:, None]
    targets = leaf_count + jnp.sum(
        jnp.where(placing, couple_dst[None, :] - leaf_count, 0), axis=1
    ).reshape(peer_count, slot_cap)
    target_rows = jnp.pad(
        targets.astype(bf16)[:, None, :], ((0, 0), (0, 15), (0, 128 - slot_cap))
    )
    outgoing = pl.pallas_call(
        functools.partial(pair_kernel, slot_cap),
        out_shape=jax.ShapeDtypeStruct((peer_count, slot_cap * 8 + 16, 128), bf16),
        in_specs=[SM, SM, VM, VM, VM],
        out_specs=VM,
        scratch_shapes=[pltpu.VMEM((slot_total * 8, 128), f32), spread_shape],
        compiler_params=CP,
        cost_estimate=pl.CostEstimate(flops=10**9, bytes_accessed=4 * 10**7, transcendentals=0),
        name="pairs",
    )(couple_src, slot_ids, coeff_round, couple_blocks, target_rows)
    arrived = lax.all_to_all(outgoing, "leaf", split_axis=0, concat_axis=0, tiled=True)
    arrived_targets = arrived[:, slot_cap * 8, :slot_cap].astype(jnp.int32).reshape(slot_total)

    top_tiers = peer_count.bit_length() - 1
    edge_mats = top_edges[0].reshape(top_tiers - 1, RANK, RANK)
    couple_mats = top_couple[0].reshape(top_tiers, RANK, RANK)
    current = root_coeff
    sibling_list = []
    for section_no in range(top_tiers - 1):
        own_part = jnp.dot(current, edge_mats[section_no], precision=exact_prec)
        both = partner(jnp.concatenate([current, own_part], axis=1), "leaf", section_no)
        sibling_list.append(both[:, :RANK])
        current = own_part + both[:, RANK:]
    sibling_list.append(partner(current, "leaf", top_tiers - 1))
    downward = jnp.dot(
        sibling_list[top_tiers - 1], couple_mats[top_tiers - 1].T, precision=exact_prec
    )
    for section_no in reversed(range(top_tiers - 1)):
        coupled = jnp.dot(sibling_list[section_no], couple_mats[section_no].T, precision=exact_prec)
        downward = coupled + jnp.dot(downward, edge_mats[section_no].T, precision=exact_prec)

    forward = [(i, (i + 1) % peer_count) for i in range(peer_count)]
    backward = [(target, source) for source, target in forward]
    low = lax.ppermute(x_vecs[:, -LEAF:], "leaf", forward)
    high = lax.ppermute(x_vecs[:, :LEAF], "leaf", backward)
    leaf_down, near_part = pl.pallas_call(
        down_kernel,
        out_shape=(
            jax.ShapeDtypeStruct((points, RANK), f32),
            jax.ShapeDtypeStruct((points, RANK), f32),
        ),
        in_specs=[VM] * 6,
        out_specs=(VM, VM),
        scratch_shapes=[pltpu.VMEM((points + 2 * NV, RANK), bf16), spread_shape],
        compiler_params=CP,
        cost_estimate=pl.CostEstimate(flops=10**10, bytes_accessed=10**8, transcendentals=0),
        name="down",
    )(downward, local_edges, x_vecs, low, high, near_blocks)

    acc_shape = pltpu.VMEM((leaf_count * 8 + 8, 128), f32)
    return pl.pallas_call(
        final_kernel,
        out_shape=jax.ShapeDtypeStruct((NV, leaf_count * LEAF), f32),
        in_specs=[SM, VM, VM, VM, VM],
        out_specs=VM,
        scratch_shapes=[acc_shape] * 4 + [spread_shape],
        compiler_params=CP,
        name="final",
    )(arrived_targets, arrived, leaf_down, near_part, leaf_basis)


def solution(mesh):
    return jax.shard_map(
        shards,
        mesh=mesh,
        in_specs=(
            P(None, "leaf"),
            P("leaf", None),
            P("leaf", None),
            P("leaf", None),
            P("leaf", None, None),
            P("leaf", None, None),
            P("leaf", None),
            P("leaf"),
            P("leaf", None),
            P("leaf"),
        ),
        out_specs=P(None, "leaf"),
        check_vma=False,
    )
```
